32 devices in a mesh: dp: 16 (over z, x, core), bfly: 2 (over y).
Axes of the slice: x: 2, y: 2, z: 4, core: 2. Of those that a mesh axis runs over, the one named last changes fastest.
Arguments:
- features: bfloat16 [2048, 8192], P('dp', 'bfly'), may hold values from -6 to 6
- weight: bfloat16 [4, 256, 14336], P(None, 'dp', 'bfly'), may hold values from -0.1875 to 0.1875
- block_table: int32 [4, 56], P(None, 'bfly'), may hold values from 0 to 15
- upstream: bfloat16 [2048, 14336], P('dp', 'bfly'), may hold values from -6 to 6
Outputs:
- activation: bfloat16 [2048, 14336], P('dp', 'bfly')
- input_grad: bfloat16 [2048, 8192], P('dp', 'bfly')
- weight_grad: float32 [4, 256, 14336], P(None, 'dp', 'bfly')
The draws below stay inside these ranges and needn't reach their ends.
Inputs may be any that keep to these rules, and one draw needn't show every extreme that they name: block_table[s, k] names a feature block within the partner group of hidden block k at section s.
All inputs are finite; a program needn't handle non-finite values.
Results may differ from the reference program's by a relative error of at most 0.0058.
Values may be sent and summed in bfloat16 or wider, within the bound.
A program may use at most 128 MiB of HBM per device.

```python
import jax
import jax.numpy as jnp
from jax import lax

D = 8192
FF = 14336
BLK = 256
SECTIONS = 4
TOKENS = 2048
FBLK = 16
HBLK = 56
N_BFLY = 2


def with_ends(array, key, low, top_value):
    dims = array.shape
    index_at = [jax.random.randint(jax.random.fold_in(key, axis), (), 0, dims[axis]) for axis in range(len(dims))]
    array = array.at[tuple(index_at)].set(low)
    longest = dims.index(max(dims))
    index_at[longest] = (index_at[longest] + 1) % dims[longest]
    return array.at[tuple(index_at)].set(top_value)


def level_of(key, dims, split, low, largest):
    level, own = 1.0, jax.random.fold_in(key, 6)
    for axis_at, shards_of in split:
        steps = jnp.exp(jax.random.uniform(jax.random.fold_in(own, axis_at), (shards_of,), jnp.float32, low / len(split), largest / len(split)))
        level = level * jnp.repeat(steps, dims[axis_at] // shards_of).reshape([-1 if axis == axis_at else 1 for axis in range(len(dims))])
    return level


def bell_draw(key, dims, scale, most, pieces=(), kind=jnp.bfloat16):
    result = jax.random.normal(key, dims, jnp.float32) * scale
    if len(pieces) > 0:
        result = level_of(key, dims, pieces, -0.22, 0.18) * result
    return jnp.clip(result, min=-most, max=most).astype(kind)


def setup_inputs(seed: int = 0) -> dict:
    streams_of = jax.random.split(jax.random.key(seed), 5)
    return {
        "features": bell_draw(streams_of[0], (TOKENS, D), 1.0, 6.0, ((0, 16), (1, 2))),
        "weight": bell_draw(streams_of[1], (SECTIONS, BLK, FF), (SECTIONS * BLK) ** -0.5, 0.1875, ((1, 16), (2, 2))),
        "block_table": with_ends(jax.random.randint(streams_of[2], (SECTIONS, HBLK), 0, FBLK), jax.random.fold_in(streams_of[2], 1), 0, FBLK - 1).astype(jnp.int32),
        "upstream": bell_draw(streams_of[3], (TOKENS, FF), 1.0, 6.0, ((0, 16), (1, 2))),
    }


half_root = 0.7071067811865476
inv_root_tau = 0.3989422804014327


def gelu_pair(pre_act):
    normal_cdf = 0.5 * (1.0 + lax.erf(pre_act * half_root))
    density = jnp.exp(-0.5 * pre_act * pre_act) * inv_root_tau
    return pre_act * normal_cdf, normal_cdf + pre_act * density


def reference(features, weight, block_table, upstream):
    tokens = features.shape[0]
    feat_blocks = D // (BLK * N_BFLY)
    hidden_group = FF // (BLK * N_BFLY)
    bit_count = N_BFLY.bit_length() - 1
    own_slabs = features.reshape(tokens, N_BFLY, feat_blocks, BLK)
    weights = weight.reshape(SECTIONS, BLK, N_BFLY, hidden_group, BLK).astype(jnp.float32)
    table = block_table.reshape(SECTIONS, N_BFLY, hidden_group)
    cotangent = upstream.reshape(tokens, N_BFLY, hidden_group, BLK).astype(jnp.float32)
    columns = jnp.arange(feat_blocks, dtype=jnp.int32)
    grad_scale = float(tokens) ** -0.5
    activations = []
    gradients = []
    input_grad = jnp.zeros((tokens, N_BFLY, feat_blocks, BLK), jnp.float32)
    for own_group in range(N_BFLY):
        partners = [own_group] + [own_group ^ (1 << ((section_index - 1) % bit_count)) for section_index in range(1, SECTIONS)]
        gathered = jnp.stack(
            [jnp.take(own_slabs[:, partners[section_index]], table[section_index, own_group], axis=1) for section_index in range(SECTIONS)],
            axis=2).astype(jnp.float32)
        group_weight = weights[:, :, own_group]
        pre_act = jnp.einsum("tjsc,scjd->tjd", gathered, group_weight)
        activated, slope_term = gelu_pair(pre_act)
        activations.append(activated.astype(jnp.bfloat16))
        grad_low = lax.optimization_barrier((cotangent[:, own_group] * slope_term).astype(jnp.bfloat16))
        grad_pre = grad_low.astype(jnp.float32)
        gradients.append(jnp.einsum("tjsc,tjd->scjd", gathered, grad_pre) * grad_scale)
        back_terms = jnp.einsum("tjd,scjd->tjsc", grad_pre, group_weight)
        shares = {}
        for section_index in range(SECTIONS):
            onehot = (table[section_index, own_group][:, None] == columns[None, :]).astype(jnp.float32)
            placed = jnp.einsum("jb,tjc->tbc", onehot, back_terms[:, :, section_index],
                                precision=lax.Precision.HIGHEST)
            target = partners[section_index]
            shares[target] = placed if target not in shares else shares[target] + placed
        for target in shares:
            rounded = lax.optimization_barrier(shares[target].astype(jnp.bfloat16))
            input_grad = input_grad.at[:, target].add(rounded.astype(jnp.float32))
    activation = jnp.stack(activations, axis=1).reshape(tokens, FF)
    weight_grad = jnp.stack(gradients, axis=2).reshape(SECTIONS, BLK, FF)
    return activation, input_grad.reshape(tokens, D).astype(jnp.bfloat16), weight_grad
```

```python
import functools

import jax
import jax.numpy as jnp
from jax import lax
from jax.experimental import pallas as pl
from jax.experimental.pallas import tpu as pltpu
from jax.sharding import PartitionSpec as P

half_root = 0.7071067811865476
inv_root_tau = 0.3989422804014327
MESH = pl.DeviceIdType.MESH
CHIPS = 8
PARTS = 4
VMEM = pl.BlockSpec(memory_space=pltpu.VMEM)
ANY = pl.BlockSpec(memory_space=pl.ANY)


def swapped(block, axis, stride):
    count = lax.axis_size(axis)
    route = []
    for low in range(count):
        high = low | 1 << stride
        if high != low and high < count:
            route += [(low, high), (high, low)]
    return lax.ppermute(block, axis, route)


def gelu_pair(pre_act):
    normal_cdf = 0.5 * (1.0 + lax.erf(pre_act * half_root))
    density = jnp.exp(-0.5 * pre_act * pre_act) * inv_root_tau
    return (pre_act * normal_cdf, normal_cdf + pre_act * density)


def ring_place():
    dp = lax.axis_index("dp")
    z, x, core = dp // 4, (dp // 2) % 2, dp % 2
    return z + x * (7 - 2 * z), core


def ring_member(place, core):
    place = lax.rem(place + 2 * CHIPS, CHIPS)
    side = place // 4
    return (place + side * (7 - 2 * place)) * 4 + 2 * side + core


def greet(place, core):
    fly = lax.axis_index("bfly")
    barrier = pltpu.get_barrier_semaphore()
    friends = [
        (ring_member(place + 1, core), fly),
        (ring_member(place - 1, core), fly),
        (ring_member(place, 1 - core), fly),
        (ring_member(place, core), 1 - fly),
    ]
    for friend in friends:
        pl.semaphore_signal(barrier, inc=1, device_id=friend, device_id_type=MESH)
    pl.semaphore_wait(barrier, 4)
    return friends


def remote(src, dst, send, recv, where):
    return pltpu.make_async_remote_copy(
        src_ref=src, dst_ref=dst, send_sem=send, recv_sem=recv, device_id=where, device_id_type=MESH
    )


def gather_kernel(w_ref, feat_ref, all_ref, other_ref, own_sem, fly_sem, ring_sem, sib_sem):
    place, core = ring_place()
    up, down, sibling, across = greet(place, core)
    half, width = w_ref.shape[0] // 2, w_ref.shape[1]
    cols = width // PARTS
    fly = remote(feat_ref, other_ref, fly_sem.at[0], fly_sem.at[1], across)
    fly.start()
    own = pltpu.make_async_copy(w_ref, all_ref.at[ring_member(place, core)], own_sem)
    own.start()
    own.wait()

    def view(owner_place, way, part, owner_core):
        return all_ref.at[
            ring_member(owner_place, owner_core), pl.ds(way * half, half), pl.ds(part * cols, cols)
        ]

    def ring(step, way, part):
        piece = view(place - step if way == 0 else place + step, way, part, core)
        return remote(
            piece, piece, ring_sem.at[0, way, part, step], ring_sem.at[1, way, part, step],
            up if way == 0 else down,
        )

    def sib(step, way, part):
        piece = view(place - step if way == 0 else place + step, way, part, core)
        return remote(
            piece, piece, sib_sem.at[0, way, part, step], sib_sem.at[1, way, part, step], sibling
        )

    def at_step(step, carry):
        for part in range(PARTS):
            for way in range(2):
                pl.when(step > 0)(lambda: ring(step - 1, way, part).wait_recv())
                pl.when(step < CHIPS - 1)(lambda: ring(step, way, part).start())
                sib(step, way, part).start()
        return carry

    lax.fori_loop(0, CHIPS, at_step, 0)

    def finish(step, carry):
        for part in range(PARTS):
            for way in range(2):
                pl.when(step < CHIPS - 1)(lambda: ring(step, way, part).wait_send())
                sib(step, way, part).wait()
        return carry

    lax.fori_loop(0, CHIPS, finish, 0)
    fly.wait()


def gather_weights(blob, features):
    rows, width = blob.shape
    return pl.pallas_call(
        gather_kernel,
        name="gather_weights",
        out_shape=(
            jax.ShapeDtypeStruct((2 * CHIPS, rows, width), blob.dtype),
            jax.ShapeDtypeStruct(features.shape, features.dtype),
        ),
        in_specs=[ANY, ANY],
        out_specs=(ANY, ANY),
        scratch_shapes=[
            pltpu.SemaphoreType.DMA,
            pltpu.SemaphoreType.DMA((2,)),
            pltpu.SemaphoreType.DMA((2, 2, PARTS, CHIPS)),
            pltpu.SemaphoreType.DMA((2, 2, PARTS, CHIPS)),
        ],
        compiler_params=pltpu.CompilerParams(collective_id=0, has_side_effects=True),
    )(blob, features)


def scatter_kernel(
    g_ref, shares_ref, out_ref, grad_ref, mine, theirs, arrived, far_share, load_sem, fly_sem, ring_sem, sib_sem
):
    place, core = ring_place()
    up, down, sibling, across = greet(place, core)
    half, width = mine.shape[2], mine.shape[3]
    cols = width // PARTS
    fly = remote(shares_ref.at[1], far_share, fly_sem.at[0], fly_sem.at[1], across)

    def target(step, way):
        return place - 1 - step if way == 0 else place + 1 + step

    def span(part):
        return pl.ds(part * cols, cols)

    def load(step, way, part):
        return pltpu.make_async_copy(
            g_ref.at[ring_member(target(step, way), core), pl.ds(way * half, half), span(part)],
            mine.at[way, step, :, span(part)],
            load_sem.at[way, part, step],
        )

    def sib(step, way, part):
        return remote(
            g_ref.at[ring_member(target(step, way), 1 - core), pl.ds(way * half, half), span(part)],
            theirs.at[way, step, :, span(part)],
            sib_sem.at[0, way, part, step],
            sib_sem.at[1, way, part, step],
            sibling,
        )

    def ring(step, way, part):
        return remote(
            mine.at[way, step, :, span(part)],
            arrived.at[way, step, :, span(part)],
            ring_sem.at[0, way, part, step],
            ring_sem.at[1, way, part, step],
            up if way == 0 else down,
        )

    def begin(step, carry):
        for part in range(PARTS):
            for way in range(2):
                sib(step, way, part).start()
                load(step, way, part).start()
        return carry

    lax.fori_loop(0, CHIPS, begin, 0)
    fly.start()

    def wide(ref, way, step, row, part):
        return ref[way, step, pl.ds(row * 16, 16), span(part)].astype(jnp.float32)

    def at_step(step, carry):
        for part in range(PARTS):
            for way in range(2):
                load(step, way, part).wait()
                sib(step, way, part).wait_recv()

                @pl.when(step == 0)
                def _():
                    for row in range(half // 16):
                        total = wide(mine, way, step, row, part) + wide(theirs, way, step, row, part)
                        mine[way, step, pl.ds(row * 16, 16), span(part)] = total.astype(mine.dtype)

                @pl.when(step > 0)
                def _():
                    ring(step - 1, way, part).wait_recv()

                @pl.when(jnp.logical_and(step > 0, step < CHIPS - 1))
                def _():
                    for row in range(half // 16):
                        total = wide(mine, way, step, row, part) + wide(theirs, way, step, row, part)
                        total = total + wide(arrived, way, step - 1, row, part)
                        mine[way, step, pl.ds(row * 16, 16), span(part)] = total.astype(mine.dtype)

                @pl.when(step < CHIPS - 1)
                def _():
                    ring(step, way, part).start()

        return carry

    lax.fori_loop(0, CHIPS, at_step, 0)
    last = CHIPS - 1
    for part in range(PARTS):
        for way in range(2):
            for row in range(half // 16):
                total = wide(mine, way, last, row, part) + wide(theirs, way, last, row, part)
                total = total + wide(arrived, way, last - 1, row, part)
                out_ref[pl.ds(way * half + row * 16, 16), span(part)] = total
    fly.wait()
    grad_ref[...] = (
        shares_ref[0].astype(jnp.float32) + far_share[...].astype(jnp.float32)
    ).astype(grad_ref.dtype)

    def finish(step, carry):
        for part in range(PARTS):
            for way in range(2):
                pl.when(step < CHIPS - 1)(lambda: ring(step, way, part).wait_send())
                sib(step, way, part).wait_send()
        return carry

    lax.fori_loop(0, CHIPS, finish, 0)


def scatter_grads(grads, shares):
    count, rows, width = grads.shape
    half = rows // 2
    return pl.pallas_call(
        scatter_kernel,
        name="scatter_grads",
        out_shape=(
            jax.ShapeDtypeStruct((rows, width), jnp.float32),
            jax.ShapeDtypeStruct(shares.shape[1:], shares.dtype),
        ),
        in_specs=[ANY, VMEM],
        out_specs=(VMEM, VMEM),
        scratch_shapes=[
            pltpu.VMEM((2, CHIPS, half, width), grads.dtype),
            pltpu.VMEM((2, CHIPS, half, width), grads.dtype),
            pltpu.VMEM((2, CHIPS - 1, half, width), grads.dtype),
            pltpu.VMEM(shares.shape[1:], shares.dtype),
            pltpu.SemaphoreType.DMA((2, PARTS, CHIPS)),
            pltpu.SemaphoreType.DMA((2,)),
            pltpu.SemaphoreType.DMA((2, 2, PARTS, CHIPS)),
            pltpu.SemaphoreType.DMA((2, 2, PARTS, CHIPS)),
        ],
        compiler_params=pltpu.CompilerParams(
            collective_id=1, has_side_effects=True, vmem_limit_bytes=48 * 2**20
        ),
    )(grads, shares)


def block_kernel(source_of, scale, table_ref, *refs):
    sources = max(source_of) + 1
    feats = refs[:sources]
    w_ref, up_ref, act_ref, g_ref, share_ref, total = refs[sources:]
    sections = len(source_of)
    count, rows = w_ref.shape[0], w_ref.shape[1] // sections
    block = w_ref.shape[2]
    k = pl.program_id(0)

    @pl.when(k == 0)
    def _():
        total[...] = jnp.zeros_like(total)

    spans = [pl.ds(pl.multiple_of(table_ref[s, k] * block, block), block) for s in range(sections)]
    taken = [feats[source_of[s]][:, spans[s]] for s in range(sections)]
    weights = [w_ref[:, s * rows : (s + 1) * rows, :].reshape(-1, block) for s in range(sections)]
    pre_act = jnp.dot(taken[0], weights[0], preferred_element_type=jnp.float32)
    for s in range(1, sections):
        pre_act = pre_act + jnp.dot(taken[s], weights[s], preferred_element_type=jnp.float32)
    activated, slope = gelu_pair(pre_act)
    act_ref[...] = activated.astype(act_ref.dtype)
    grad_pre = (up_ref[...].astype(jnp.float32) * slope).astype(jnp.bfloat16)
    for s in range(sections):
        back = lax.dot_general(
            grad_pre, weights[s], (((1,), (1,)), ((), ())), preferred_element_type=jnp.float32
        )
        total[source_of[s], :, spans[s]] += back
        grad = lax.dot_general(
            taken[s], grad_pre, (((0,), (0,)), ((), ())), preferred_element_type=jnp.float32
        )
        g_ref[:, s * rows : (s + 1) * rows, :] = (grad * scale).astype(g_ref.dtype).reshape(
            count, rows, block
        )

    @pl.when(k == pl.num_programs(0) - 1)
    def _():
        share_ref[...] = total[...].astype(share_ref.dtype)


def block_math(source_of, scale, table, feats, w_all, upstream):
    tok_rows, width = upstream.shape
    count, rows, _ = w_all.shape
    hidden = table.shape[1]
    block = width // hidden
    wide = feats[0].shape[1]
    sources = len(feats)
    flops = 2 * 3 * tok_rows * width * count * rows
    return pl.pallas_call(
        functools.partial(block_kernel, source_of, scale),
        name="block_math",
        grid_spec=pltpu.PrefetchScalarGridSpec(
            num_scalar_prefetch=1,
            grid=(hidden,),
            in_specs=[pl.BlockSpec((tok_rows, wide), lambda k, t: (0, 0))] * sources
            + [
                pl.BlockSpec((count, rows, block), lambda k, t: (0, 0, k)),
                pl.BlockSpec((tok_rows, block), lambda k, t: (0, k)),
            ],
            out_specs=[
                pl.BlockSpec((tok_rows, block), lambda k, t: (0, k)),
                pl.BlockSpec((count, rows, block), lambda k, t: (0, 0, k)),
                pl.BlockSpec((sources, tok_rows, wide), lambda k, t: (0, 0, 0)),
            ],
            scratch_shapes=[pltpu.VMEM((sources, tok_rows, wide), jnp.float32)],
        ),
        out_shape=(
            jax.ShapeDtypeStruct((tok_rows, width), jnp.bfloat16),
            jax.ShapeDtypeStruct((count, rows, width), jnp.bfloat16),
            jax.ShapeDtypeStruct((sources, tok_rows, wide), jnp.bfloat16),
        ),
        compiler_params=pltpu.CompilerParams(
            dimension_semantics=("arbitrary",), vmem_limit_bytes=40 * 2**20
        ),
        cost_estimate=pl.CostEstimate(
            flops=flops, bytes_accessed=4 * count * rows * width, transcendentals=2 * tok_rows * width
        ),
    )(table, *feats, w_all, upstream)


def body(on_ring, features, weight, block_table, upstream):
    tok_rows = features.shape[0]
    sections, rows, local_width = weight.shape
    groups = lax.axis_size("bfly")
    bit_count = groups.bit_length() - 1
    data_count = lax.axis_size("dp")
    scale = float(tok_rows * data_count) ** (-0.5)
    section_bits = [(section_index - 1) % bit_count for section_index in range(1, sections)]
    used_bits = sorted(set(section_bits))
    source_of = (0,) + tuple(1 + used_bits.index(bit) for bit in section_bits)
    if on_ring:
        blob = weight.reshape(sections * rows, local_width)
        w_all, partner = gather_weights(blob, features)
        activation, grads, shares = block_math(
            source_of, scale, block_table, [features, partner], w_all, upstream
        )
        weight_grad, input_grad = scatter_grads(grads, shares)
        return (activation, input_grad, weight_grad.reshape(weight.shape))
    feats = [features] + [swapped(features, "bfly", bit) for bit in used_bits]
    w_all = lax.all_gather(weight, "dp", axis=1, tiled=True).reshape(1, -1, local_width)
    activation, grads, shares = block_math(source_of, scale, block_table, feats, w_all, upstream)
    input_grad = shares[0].astype(jnp.float32)
    for at, bit in enumerate(used_bits):
        input_grad = input_grad + swapped(shares[1 + at], "bfly", bit).astype(jnp.float32)
    weight_grad = lax.psum_scatter(
        grads.reshape(sections, -1, local_width).astype(jnp.float32), "dp", scatter_dimension=1, tiled=True
    )
    return (activation, input_grad.astype(jnp.bfloat16), weight_grad)


def solution(mesh):
    on_ring = mesh.shape["dp"] == 2 * CHIPS and mesh.shape["bfly"] == 2
    return jax.shard_map(
        functools.partial(body, on_ring),
        mesh=mesh,
        in_specs=(P("dp", "bfly"), P(None, "dp", "bfly"), P(None, "bfly"), P("dp", "bfly")),
        out_specs=(P("dp", "bfly"), P("dp", "bfly"), P(None, "dp", "bfly")),
        check_vma=False,
    )
```

```python
import functools

import jax
import jax.numpy as jnp
from jax import lax
from jax.experimental import pallas as pl
from jax.experimental.pallas import tpu as pltpu
from jax.sharding import PartitionSpec as P

half_root = 0.7071067811865476
inv_root_tau = 0.3989422804014327
MESH = pl.DeviceIdType.MESH
CHIPS = 8
LOTS = 4
PARTS = 2
VMEM = pl.BlockSpec(memory_space=pltpu.VMEM)
ANY = pl.BlockSpec(memory_space=pl.ANY)


def swapped(block, axis, stride):
    count = lax.axis_size(axis)
    route = []
    for low in range(count):
        high = low | 1 << stride
        if high != low and high < count:
            route += [(low, high), (high, low)]
    return lax.ppermute(block, axis, route)


def gelu_pair(pre_act):
    normal_cdf = 0.5 * (1.0 + lax.erf(pre_act * half_root))
    density = jnp.exp(-0.5 * pre_act * pre_act) * inv_root_tau
    return (pre_act * normal_cdf, normal_cdf + pre_act * density)


def ring_place():
    dp = lax.axis_index("dp")
    z, x, core = dp // 4, (dp // 2) % 2, dp % 2
    return z + x * (7 - 2 * z), core


def ring_member(place, core):
    place = lax.rem(place + 2 * CHIPS, CHIPS)
    side = place // 4
    return (place + side * (7 - 2 * place)) * 4 + 2 * side + core


def greet(place, core):
    fly = lax.axis_index("bfly")
    barrier = pltpu.get_barrier_semaphore()
    friends = [
        (ring_member(place + 1, core), fly),
        (ring_member(place - 1, core), fly),
        (ring_member(place, 1 - core), fly),
        (ring_member(place, core), 1 - fly),
    ]
    for friend in friends:
        pl.semaphore_signal(barrier, inc=1, device_id=friend, device_id_type=MESH)
    pl.semaphore_wait(barrier, 4)
    return friends


def remote(src, dst, send, recv, where):
    return pltpu.make_async_remote_copy(
        src_ref=src, dst_ref=dst, send_sem=send, recv_sem=recv, device_id=where, device_id_type=MESH
    )


def gather_kernel(w_ref, feat_ref, all_ref, other_ref, own_sem, fly_sem, ring_sem, sib_sem):
    place, core = ring_place()
    up, down, sibling, across = greet(place, core)
    half, width = w_ref.shape[0] // 2, w_ref.shape[1]
    cols = width // PARTS
    fly = remote(feat_ref, other_ref, fly_sem.at[0], fly_sem.at[1], across)
    fly.start()
    own = pltpu.make_async_copy(w_ref, all_ref.at[ring_member(place, core)], own_sem)
    own.start()
    own.wait()

    def view(owner_place, way, part, owner_core):
        return all_ref.at[
            ring_member(owner_place, owner_core), pl.ds(way * half, half), pl.ds(part * cols, cols)
        ]

    def ring(step, way, part):
        piece = view(place - step if way == 0 else place + step, way, part, core)
        return remote(
            piece, piece, ring_sem.at[0, way, part, step], ring_sem.at[1, way, part, step],
            up if way == 0 else down,
        )

    def sib(step, way, part):
        piece = view(place - step if way == 0 else place + step, way, part, core)
        return remote(
            piece, piece, sib_sem.at[0, way, part, step], sib_sem.at[1, way, part, step], sibling
        )

    def at_step(step, carry):
        for part in range(PARTS):
            for way in range(2):
                pl.when(step > 0)(lambda: ring(step - 1, way, part).wait_recv())
                pl.when(step < CHIPS - 1)(lambda: ring(step, way, part).start())
                sib(step, way, part).start()
        return carry

    lax.fori_loop(0, CHIPS, at_step, 0)

    def finish(step, carry):
        for part in range(PARTS):
            for way in range(2):
                pl.when(step < CHIPS - 1)(lambda: ring(step, way, part).wait_send())
                sib(step, way, part).wait()
        return carry

    lax.fori_loop(0, CHIPS, finish, 0)
    fly.wait()


def gather_weights(blob, features):
    rows, width = blob.shape
    return pl.pallas_call(
        gather_kernel,
        name="gather_weights",
        out_shape=(
            jax.ShapeDtypeStruct((2 * CHIPS, rows, width), blob.dtype),
            jax.ShapeDtypeStruct(features.shape, features.dtype),
        ),
        in_specs=[ANY, ANY],
        out_specs=(VMEM, ANY),
        scratch_shapes=[
            pltpu.SemaphoreType.DMA,
            pltpu.SemaphoreType.DMA((2,)),
            pltpu.SemaphoreType.DMA((2, 2, PARTS, CHIPS)),
            pltpu.SemaphoreType.DMA((2, 2, PARTS, CHIPS)),
        ],
        compiler_params=pltpu.CompilerParams(collective_id=0, has_side_effects=True, vmem_limit_bytes=40 * 2**20),
    )(blob, features)


def scatter_kernel(
    g_ref, shares_ref, out_ref, grad_ref, mine, theirs, arrived, far_share, load_sem, fly_sem, ring_sem, sib_sem
):
    place, core = ring_place()
    up, down, sibling, across = greet(place, core)
    half, width = mine.shape[2], mine.shape[3]
    cols = width // PARTS
    fly = remote(shares_ref.at[1], far_share, fly_sem.at[0], fly_sem.at[1], across)

    def target(step, way):
        return place - 1 - step if way == 0 else place + 1 + step

    def span(part):
        return pl.ds(part * cols, cols)

    def load(step, way, part):
        return pltpu.make_async_copy(
            g_ref.at[ring_member(target(step, way), core), pl.ds(way * half, half), span(part)],
            mine.at[way, step, :, span(part)],
            load_sem.at[way, part, step],
        )

    def sib(step, way, part):
        return remote(
            g_ref.at[ring_member(target(step, way), 1 - core), pl.ds(way * half, half), span(part)],
            theirs.at[way, step, :, span(part)],
            sib_sem.at[0, way, part, step],
            sib_sem.at[1, way, part, step],
            sibling,
        )

    def ring(step, way, part):
        return remote(
            mine.at[way, step, :, span(part)],
            arrived.at[way, step, :, span(part)],
            ring_sem.at[0, way, part, step],
            ring_sem.at[1, way, part, step],
            up if way == 0 else down,
        )

    def begin(step, carry):
        for part in range(PARTS):
            for way in range(2):
                sib(step, way, part).start()
                load(step, way, part).start()
        return carry

    lax.fori_loop(0, CHIPS, begin, 0)
    fly.start()

    def wide(ref, way, step, row, part):
        return ref[way, step, pl.ds(row * 16, 16), span(part)].astype(jnp.float32)

    def at_step(step, carry):
        for part in range(PARTS):
            for way in range(2):
                load(step, way, part).wait()
                sib(step, way, part).wait_recv()

                @pl.when(step == 0)
                def _():
                    for row in range(half // 16):
                        total = wide(mine, way, step, row, part) + wide(theirs, way, step, row, part)
                        mine[way, step, pl.ds(row * 16, 16), span(part)] = total.astype(mine.dtype)

                @pl.when(step > 0)
                def _():
                    ring(step - 1, way, part).wait_recv()

                @pl.when(jnp.logical_and(step > 0, step < CHIPS - 1))
                def _():
                    for row in range(half // 16):
                        total = wide(mine, way, step, row, part) + wide(theirs, way, step, row, part)
                        total = total + wide(arrived, way, step - 1, row, part)
                        mine[way, step, pl.ds(row * 16, 16), span(part)] = total.astype(mine.dtype)

                @pl.when(step < CHIPS - 1)
                def _():
                    ring(step, way, part).start()

        return carry

    lax.fori_loop(0, CHIPS, at_step, 0)
    last = CHIPS - 1
    for part in range(PARTS):
        for way in range(2):
            for row in range(half // 16):
                total = wide(mine, way, last, row, part) + wide(theirs, way, last, row, part)
                total = total + wide(arrived, way, last - 1, row, part)
                out_ref[pl.ds(way * half + row * 16, 16), span(part)] = total
    fly.wait()
    grad_ref[...] = (
        shares_ref[0].astype(jnp.float32) + far_share[...].astype(jnp.float32)
    ).astype(grad_ref.dtype)

    def finish(step, carry):
        for part in range(PARTS):
            for way in range(2):
                pl.when(step < CHIPS - 1)(lambda: ring(step, way, part).wait_send())
                sib(step, way, part).wait_send()
        return carry

    lax.fori_loop(0, CHIPS, finish, 0)


def scatter_grads(grads, shares):
    count, rows, width = grads.shape
    half = rows // 2
    return pl.pallas_call(
        scatter_kernel,
        name="scatter_grads",
        out_shape=(
            jax.ShapeDtypeStruct((rows, width), jnp.float32),
            jax.ShapeDtypeStruct(shares.shape[1:], shares.dtype),
        ),
        in_specs=[ANY, VMEM],
        out_specs=(VMEM, VMEM),
        scratch_shapes=[
            pltpu.VMEM((2, CHIPS, half, width), grads.dtype),
            pltpu.VMEM((2, CHIPS, half, width), grads.dtype),
            pltpu.VMEM((2, CHIPS - 1, half, width), grads.dtype),
            pltpu.VMEM(shares.shape[1:], shares.dtype),
            pltpu.SemaphoreType.DMA((2, PARTS, CHIPS)),
            pltpu.SemaphoreType.DMA((2,)),
            pltpu.SemaphoreType.DMA((2, 2, PARTS, CHIPS)),
            pltpu.SemaphoreType.DMA((2, 2, PARTS, CHIPS)),
        ],
        compiler_params=pltpu.CompilerParams(
            collective_id=1, has_side_effects=True, vmem_limit_bytes=48 * 2**20
        ),
    )(grads, shares)


def block_kernel(source_of, scale, table_ref, *refs):
    sources = max(source_of) + 1
    feats = refs[:sources]
    w_ref, up_ref, act_ref, g_ref, share_ref, total, flipped = refs[sources:]
    sections = len(source_of)
    count, rows = w_ref.shape[0], w_ref.shape[1] // sections
    tokens, wide = feats[0].shape
    lots = table_ref.shape[1] // pl.num_programs(0)
    block = w_ref.shape[2] // lots
    at = pl.program_id(0)

    @pl.when(at == 0)
    def _():
        total[...] = jnp.zeros_like(total)
        for source in range(sources):
            for b in range(wide // block):
                span = slice(b * block, (b + 1) * block)
                flipped[source, span, :] = feats[source][:, span].T

    for lot in range(lots):
        k = at * lots + lot
        col = slice(lot * block, (lot + 1) * block)
        spans = [
            pl.ds(pl.multiple_of(table_ref[s, k] * block, block), block) for s in range(sections)
        ]
        weights = [
            w_ref[:, s * rows : (s + 1) * rows, col].reshape(-1, block) for s in range(sections)
        ]
        pre_act = jnp.zeros((tokens, block), jnp.float32)
        for s in range(sections):
            pre_act = pre_act + jnp.dot(
                feats[source_of[s]][:, spans[s]], weights[s], preferred_element_type=jnp.float32
            )
        activated, slope = gelu_pair(pre_act)
        act_ref[:, col] = activated.astype(act_ref.dtype)
        grad_pre = (up_ref[:, col].astype(jnp.float32) * slope).astype(jnp.bfloat16)
        for s in range(sections):
            back = lax.dot_general(
                grad_pre, weights[s], (((1,), (1,)), ((), ())), preferred_element_type=jnp.float32
            )
            total[source_of[s], :, spans[s]] += back
            grad = jnp.dot(
                flipped[source_of[s], spans[s], :], grad_pre, preferred_element_type=jnp.float32
            )
            g_ref[:, s * rows : (s + 1) * rows, col] = (
                (grad * scale).astype(g_ref.dtype).reshape(count, rows, block)
            )

    @pl.when(at == pl.num_programs(0) - 1)
    def _():
        share_ref[...] = total[...].astype(share_ref.dtype)


def block_math(source_of, scale, table, feats, w_all, upstream):
    tok_rows, width = upstream.shape
    count, rows, _ = w_all.shape
    hidden = table.shape[1]
    lots = LOTS if hidden % LOTS == 0 else 1
    span = width // hidden * lots
    wide = feats[0].shape[1]
    sources = len(feats)
    flops = 2 * 3 * tok_rows * width * count * rows
    return pl.pallas_call(
        functools.partial(block_kernel, source_of, scale),
        name="block_math",
        grid_spec=pltpu.PrefetchScalarGridSpec(
            num_scalar_prefetch=1,
            grid=(hidden // lots,),
            in_specs=[pl.BlockSpec((tok_rows, wide), lambda k, t: (0, 0))] * sources
            + [
                pl.BlockSpec((count, rows, span), lambda k, t: (0, 0, k)),
                pl.BlockSpec((tok_rows, span), lambda k, t: (0, k)),
            ],
            out_specs=[
                pl.BlockSpec((tok_rows, span), lambda k, t: (0, k)),
                pl.BlockSpec((count, rows, span), lambda k, t: (0, 0, k)),
                pl.BlockSpec((sources, tok_rows, wide), lambda k, t: (0, 0, 0)),
            ],
            scratch_shapes=[
                pltpu.VMEM((sources, tok_rows, wide), jnp.float32),
                pltpu.VMEM((sources, wide, tok_rows), jnp.bfloat16),
            ],
        ),
        out_shape=(
            jax.ShapeDtypeStruct((tok_rows, width), jnp.bfloat16),
            jax.ShapeDtypeStruct((count, rows, width), jnp.bfloat16),
            jax.ShapeDtypeStruct((sources, tok_rows, wide), jnp.bfloat16),
        ),
        compiler_params=pltpu.CompilerParams(
            dimension_semantics=("arbitrary",), vmem_limit_bytes=40 * 2**20
        ),
        cost_estimate=pl.CostEstimate(
            flops=flops, bytes_accessed=4 * count * rows * width, transcendentals=2 * tok_rows * width
        ),
    )(table, *feats, w_all, upstream)


def body(on_ring, features, weight, block_table, upstream):
    tok_rows = features.shape[0]
    sections, rows, local_width = weight.shape
    groups = lax.axis_size("bfly")
    bit_count = groups.bit_length() - 1
    data_count = lax.axis_size("dp")
    scale = float(tok_rows * data_count) ** (-0.5)
    section_bits = [(section_index - 1) % bit_count for section_index in range(1, sections)]
    used_bits = sorted(set(section_bits))
    source_of = (0,) + tuple(1 + used_bits.index(bit) for bit in section_bits)
    if on_ring:
        blob = weight.reshape(sections * rows, local_width)
        w_all, partner = gather_weights(blob, features)
        activation, grads, shares = block_math(
            source_of, scale, block_table, [features, partner], w_all, upstream
        )
        weight_grad, input_grad = scatter_grads(grads, shares)
        return (activation, input_grad, weight_grad.reshape(weight.shape))
    feats = [features] + [swapped(features, "bfly", bit) for bit in used_bits]
    w_all = lax.all_gather(weight, "dp", axis=1, tiled=True).reshape(1, -1, local_width)
    activation, grads, shares = block_math(source_of, scale, block_table, feats, w_all, upstream)
    input_grad = shares[0].astype(jnp.float32)
    for at, bit in enumerate(used_bits):
        input_grad = input_grad + swapped(shares[1 + at], "bfly", bit).astype(jnp.float32)
    weight_grad = lax.psum_scatter(
        grads.reshape(sections, -1, local_width).astype(jnp.float32), "dp", scatter_dimension=1, tiled=True
    )
    return (activation, input_grad.astype(jnp.bfloat16), weight_grad)


def solution(mesh):
    on_ring = mesh.shape["dp"] == 2 * CHIPS and mesh.shape["bfly"] == 2
    return jax.shard_map(
        functools.partial(body, on_ring),
        mesh=mesh,
        in_specs=(P("dp", "bfly"), P(None, "dp", "bfly"), P(None, "bfly"), P("dp", "bfly")),
        out_specs=(P("dp", "bfly"), P("dp", "bfly"), P(None, "dp", "bfly")),
        check_vma=False,
    )
```

```python
import functools

import jax
import jax.numpy as jnp
from jax import lax
from jax.experimental import pallas as pl
from jax.experimental.pallas import tpu as pltpu
from jax.sharding import PartitionSpec as P

half_root = 0.7071067811865476
inv_root_tau = 0.3989422804014327
MESH = pl.DeviceIdType.MESH
CHIPS = 8
LOTS = 4
PARTS = 2
VMEM = pl.BlockSpec(memory_space=pltpu.VMEM)
ANY = pl.BlockSpec(memory_space=pl.ANY)


def swapped(block, axis, stride):
    count = lax.axis_size(axis)
    route = []
    for low in range(count):
        high = low | 1 << stride
        if high != low and high < count:
            route += [(low, high), (high, low)]
    return lax.ppermute(block, axis, route)


def gelu_pair(pre_act):
    normal_cdf = 0.5 * (1.0 + lax.erf(pre_act * half_root))
    density = jnp.exp(-0.5 * pre_act * pre_act) * inv_root_tau
    return (pre_act * normal_cdf, normal_cdf + pre_act * density)


def ring_place():
    dp = lax.axis_index("dp")
    z, x, core = dp // 4, (dp // 2) % 2, dp % 2
    return z + x * (7 - 2 * z), core


def ring_member(place, core):
    place = lax.rem(place + 2 * CHIPS, CHIPS)
    side = place // 4
    return (place + side * (7 - 2 * place)) * 4 + 2 * side + core


def greet(place, core):
    fly = lax.axis_index("bfly")
    barrier = pltpu.get_barrier_semaphore()
    friends = [
        (ring_member(place + 1, core), fly),
        (ring_member(place - 1, core), fly),
        (ring_member(place, 1 - core), fly),
        (ring_member(place, core), 1 - fly),
    ]
    for friend in friends:
        pl.semaphore_signal(barrier, inc=1, device_id=friend, device_id_type=MESH)
    pl.semaphore_wait(barrier, 4)
    return friends


def remote(src, dst, send, recv, where):
    return pltpu.make_async_remote_copy(
        src_ref=src, dst_ref=dst, send_sem=send, recv_sem=recv, device_id=where, device_id_type=MESH
    )


def gather_kernel(w_ref, feat_ref, all_ref, other_ref, held, own_sem, fly_sem, ring_sem, sib_sem, out_sem):
    place, core = ring_place()
    up, down, sibling, across = greet(place, core)
    half, width = w_ref.shape[0] // 2, w_ref.shape[1]
    cols = width // PARTS
    fly = remote(feat_ref, other_ref, fly_sem.at[0], fly_sem.at[1], across)
    fly.start()
    own = pltpu.make_async_copy(w_ref, held.at[ring_member(place, core)], own_sem)
    own.start()
    own.wait()

    def view(owner_place, way, part, owner_core, ref=held):
        return ref.at[
            ring_member(owner_place, owner_core), pl.ds(way * half, half), pl.ds(part * cols, cols)
        ]

    def ring(step, way, part):
        piece = view(place - step if way == 0 else place + step, way, part, core)
        return remote(
            piece, piece, ring_sem.at[0, way, part, step], ring_sem.at[1, way, part, step],
            up if way == 0 else down,
        )

    def sib(step, way, part):
        piece = view(place - step if way == 0 else place + step, way, part, core)
        return remote(
            piece, piece, sib_sem.at[0, way, part, step], sib_sem.at[1, way, part, step], sibling
        )

    def out(step, way, part, other):
        owner = place - step if way == 0 else place + step
        owner_core = 1 - core if other else core
        return pltpu.make_async_copy(
            view(owner, way, part, owner_core),
            view(owner, way, part, owner_core, all_ref),
            out_sem.at[other, way, part, step],
        )

    def from_sibling(step, way, part):
        sib(step, way, part).wait_recv()
        out(step, way, part, 1).start()

    def at_step(step, carry):
        for part in range(PARTS):
            for way in range(2):
                pl.when(step > 0)(lambda: ring(step - 1, way, part).wait_recv())
                pl.when(step < CHIPS - 1)(lambda: ring(step, way, part).start())
                sib(step, way, part).start()
                out(step, way, part, 0).start()
                pl.when(step >= 2)(lambda: from_sibling(step - 2, way, part))
        return carry

    lax.fori_loop(0, CHIPS, at_step, 0)
    for step in (CHIPS - 2, CHIPS - 1):
        for part in range(PARTS):
            for way in range(2):
                from_sibling(step, way, part)

    def finish(step, carry):
        for part in range(PARTS):
            for way in range(2):
                pl.when(step < CHIPS - 1)(lambda: ring(step, way, part).wait_send())
                sib(step, way, part).wait_send()
                out(step, way, part, 0).wait()
                out(step, way, part, 1).wait()
        return carry

    lax.fori_loop(0, CHIPS, finish, 0)
    fly.wait()


def gather_weights(blob, features):
    rows, width = blob.shape
    return pl.pallas_call(
        gather_kernel,
        name="gather_weights",
        out_shape=(
            jax.ShapeDtypeStruct((2 * CHIPS, rows, width), blob.dtype),
            jax.ShapeDtypeStruct(features.shape, features.dtype),
        ),
        in_specs=[ANY, ANY],
        out_specs=(ANY, ANY),
        scratch_shapes=[
            pltpu.VMEM((2 * CHIPS, rows, width), blob.dtype),
            pltpu.SemaphoreType.DMA,
            pltpu.SemaphoreType.DMA((2,)),
            pltpu.SemaphoreType.DMA((2, 2, PARTS, CHIPS)),
            pltpu.SemaphoreType.DMA((2, 2, PARTS, CHIPS)),
            pltpu.SemaphoreType.DMA((2, 2, PARTS, CHIPS)),
        ],
        compiler_params=pltpu.CompilerParams(collective_id=0, has_side_effects=True, vmem_limit_bytes=40 * 2**20),
    )(blob, features)


def scatter_kernel(
    g_ref, shares_ref, out_ref, grad_ref, mine, theirs, arrived, far_share, load_sem, fly_sem, ring_sem, sib_sem
):
    place, core = ring_place()
    up, down, sibling, across = greet(place, core)
    half, width = mine.shape[2], mine.shape[3]
    cols = width // PARTS
    fly = remote(shares_ref.at[1], far_share, fly_sem.at[0], fly_sem.at[1], across)

    def target(step, way):
        return place - 1 - step if way == 0 else place + 1 + step

    def span(part):
        return pl.ds(part * cols, cols)

    def load(step, way, part):
        return pltpu.make_async_copy(
            g_ref.at[ring_member(target(step, way), core), pl.ds(way * half, half), span(part)],
            mine.at[way, step, :, span(part)],
            load_sem.at[way, part, step],
        )

    def sib(step, way, part):
        return remote(
            g_ref.at[ring_member(target(step, way), 1 - core), pl.ds(way * half, half), span(part)],
            theirs.at[way, step, :, span(part)],
            sib_sem.at[0, way, part, step],
            sib_sem.at[1, way, part, step],
            sibling,
        )

    def ring(step, way, part):
        return remote(
            mine.at[way, step, :, span(part)],
            arrived.at[way, step, :, span(part)],
            ring_sem.at[0, way, part, step],
            ring_sem.at[1, way, part, step],
            up if way == 0 else down,
        )

    def begin(step, carry):
        for part in range(PARTS):
            for way in range(2):
                sib(step, way, part).start()
                load(step, way, part).start()
        return carry

    lax.fori_loop(0, CHIPS, begin, 0)
    fly.start()

    def wide(ref, way, step, row, part):
        return ref[way, step, pl.ds(row * 16, 16), span(part)].astype(jnp.float32)

    def at_step(step, carry):
        for part in range(PARTS):
            for way in range(2):
                load(step, way, part).wait()
                sib(step, way, part).wait_recv()

                @pl.when(step == 0)
                def _():
                    for row in range(half // 16):
                        total = wide(mine, way, step, row, part) + wide(theirs, way, step, row, part)
                        mine[way, step, pl.ds(row * 16, 16), span(part)] = total.astype(mine.dtype)

                @pl.when(step > 0)
                def _():
                    ring(step - 1, way, part).wait_recv()

                @pl.when(jnp.logical_and(step > 0, step < CHIPS - 1))
                def _():
                    for row in range(half // 16):
                        total = wide(mine, way, step, row, part) + wide(theirs, way, step, row, part)
                        total = total + wide(arrived, way, step - 1, row, part)
                        mine[way, step, pl.ds(row * 16, 16), span(part)] = total.astype(mine.dtype)

                @pl.when(step < CHIPS - 1)
                def _():
                    ring(step, way, part).start()

        return carry

    lax.fori_loop(0, CHIPS, at_step, 0)
    last = CHIPS - 1
    for part in range(PARTS):
        for way in range(2):
            for row in range(half // 16):
                total = wide(mine, way, last, row, part) + wide(theirs, way, last, row, part)
                total = total + wide(arrived, way, last - 1, row, part)
                out_ref[pl.ds(way * half + row * 16, 16), span(part)] = total
    fly.wait()
    grad_ref[...] = (
        shares_ref[0].astype(jnp.float32) + far_share[...].astype(jnp.float32)
    ).astype(grad_ref.dtype)

    def finish(step, carry):
        for part in range(PARTS):
            for way in range(2):
                pl.when(step < CHIPS - 1)(lambda: ring(step, way, part).wait_send())
                sib(step, way, part).wait_send()
        return carry

    lax.fori_loop(0, CHIPS, finish, 0)


def scatter_grads(grads, shares):
    count, rows, width = grads.shape
    half = rows // 2
    return pl.pallas_call(
        scatter_kernel,
        name="scatter_grads",
        out_shape=(
            jax.ShapeDtypeStruct((rows, width), jnp.float32),
            jax.ShapeDtypeStruct(shares.shape[1:], shares.dtype),
        ),
        in_specs=[ANY, VMEM],
        out_specs=(VMEM, VMEM),
        scratch_shapes=[
            pltpu.VMEM((2, CHIPS, half, width), grads.dtype),
            pltpu.VMEM((2, CHIPS, half, width), grads.dtype),
            pltpu.VMEM((2, CHIPS - 1, half, width), grads.dtype),
            pltpu.VMEM(shares.shape[1:], shares.dtype),
            pltpu.SemaphoreType.DMA((2, PARTS, CHIPS)),
            pltpu.SemaphoreType.DMA((2,)),
            pltpu.SemaphoreType.DMA((2, 2, PARTS, CHIPS)),
            pltpu.SemaphoreType.DMA((2, 2, PARTS, CHIPS)),
        ],
        compiler_params=pltpu.CompilerParams(
            collective_id=1, has_side_effects=True, vmem_limit_bytes=48 * 2**20
        ),
    )(grads, shares)


def block_kernel(source_of, scale, table_ref, *refs):
    sources = max(source_of) + 1
    feats = refs[:sources]
    w_ref, up_ref, act_ref, g_ref, share_ref, total, flipped = refs[sources:]
    sections = len(source_of)
    count, rows = w_ref.shape[0], w_ref.shape[1] // sections
    tokens, wide = feats[0].shape
    lots = table_ref.shape[1] // pl.num_programs(0)
    block = w_ref.shape[2] // lots
    at = pl.program_id(0)

    @pl.when(at == 0)
    def _():
        total[...] = jnp.zeros_like(total)
        for source in range(sources):
            for b in range(wide // block):
                span = slice(b * block, (b + 1) * block)
                flipped[source, span, :] = feats[source][:, span].T

    for lot in range(lots):
        k = at * lots + lot
        col = slice(lot * block, (lot + 1) * block)
        spans = [
            pl.ds(pl.multiple_of(table_ref[s, k] * block, block), block) for s in range(sections)
        ]
        weights = [
            w_ref[:, s * rows : (s + 1) * rows, col].reshape(-1, block) for s in range(sections)
        ]
        pre_act = jnp.zeros((tokens, block), jnp.float32)
        for s in range(sections):
            pre_act = pre_act + jnp.dot(
                feats[source_of[s]][:, spans[s]], weights[s], preferred_element_type=jnp.float32
            )
        activated, slope = gelu_pair(pre_act)
        act_ref[:, col] = activated.astype(act_ref.dtype)
        grad_pre = (up_ref[:, col].astype(jnp.float32) * slope).astype(jnp.bfloat16)
        for s in range(sections):
            back = lax.dot_general(
                grad_pre, weights[s], (((1,), (1,)), ((), ())), preferred_element_type=jnp.float32
            )
            total[source_of[s], :, spans[s]] += back
            grad = jnp.dot(
                flipped[source_of[s], spans[s], :], grad_pre, preferred_element_type=jnp.float32
            )
            g_ref[:, s * rows : (s + 1) * rows, col] = (
                (grad * scale).astype(g_ref.dtype).reshape(count, rows, block)
            )

    @pl.when(at == pl.num_programs(0) - 1)
    def _():
        share_ref[...] = total[...].astype(share_ref.dtype)


def block_math(source_of, scale, table, feats, w_all, upstream):
    tok_rows, width = upstream.shape
    count, rows, _ = w_all.shape
    hidden = table.shape[1]
    lots = LOTS if hidden % LOTS == 0 else 1
    span = width // hidden * lots
    wide = feats[0].shape[1]
    sources = len(feats)
    flops = 2 * 3 * tok_rows * width * count * rows
    return pl.pallas_call(
        functools.partial(block_kernel, source_of, scale),
        name="block_math",
        grid_spec=pltpu.PrefetchScalarGridSpec(
            num_scalar_prefetch=1,
            grid=(hidden // lots,),
            in_specs=[pl.BlockSpec((tok_rows, wide), lambda k, t: (0, 0))] * sources
            + [
                pl.BlockSpec((count, rows, span), lambda k, t: (0, 0, k)),
                pl.BlockSpec((tok_rows, span), lambda k, t: (0, k)),
            ],
            out_specs=[
                pl.BlockSpec((tok_rows, span), lambda k, t: (0, k)),
                pl.BlockSpec((count, rows, span), lambda k, t: (0, 0, k)),
                pl.BlockSpec((sources, tok_rows, wide), lambda k, t: (0, 0, 0)),
            ],
            scratch_shapes=[
                pltpu.VMEM((sources, tok_rows, wide), jnp.float32),
                pltpu.VMEM((sources, wide, tok_rows), jnp.bfloat16),
            ],
        ),
        out_shape=(
            jax.ShapeDtypeStruct((tok_rows, width), jnp.bfloat16),
            jax.ShapeDtypeStruct((count, rows, width), jnp.bfloat16),
            jax.ShapeDtypeStruct((sources, tok_rows, wide), jnp.bfloat16),
        ),
        compiler_params=pltpu.CompilerParams(
            dimension_semantics=("arbitrary",), vmem_limit_bytes=40 * 2**20
        ),
        cost_estimate=pl.CostEstimate(
            flops=flops, bytes_accessed=4 * count * rows * width, transcendentals=2 * tok_rows * width
        ),
    )(table, *feats, w_all, upstream)


def body(on_ring, features, weight, block_table, upstream):
    tok_rows = features.shape[0]
    sections, rows, local_width = weight.shape
    groups = lax.axis_size("bfly")
    bit_count = groups.bit_length() - 1
    data_count = lax.axis_size("dp")
    scale = float(tok_rows * data_count) ** (-0.5)
    section_bits = [(section_index - 1) % bit_count for section_index in range(1, sections)]
    used_bits = sorted(set(section_bits))
    source_of = (0,) + tuple(1 + used_bits.index(bit) for bit in section_bits)
    if on_ring:
        blob = weight.reshape(sections * rows, local_width)
        w_all, partner = gather_weights(blob, features)
        activation, grads, shares = block_math(
            source_of, scale, block_table, [features, partner], w_all, upstream
        )
        weight_grad, input_grad = scatter_grads(grads, shares)
        return (activation, input_grad, weight_grad.reshape(weight.shape))
    feats = [features] + [swapped(features, "bfly", bit) for bit in used_bits]
    w_all = lax.all_gather(weight, "dp", axis=1, tiled=True).reshape(1, -1, local_width)
    activation, grads, shares = block_math(source_of, scale, block_table, feats, w_all, upstream)
    input_grad = shares[0].astype(jnp.float32)
    for at, bit in enumerate(used_bits):
        input_grad = input_grad + swapped(shares[1 + at], "bfly", bit).astype(jnp.float32)
    weight_grad = lax.psum_scatter(
        grads.reshape(sections, -1, local_width).astype(jnp.float32), "dp", scatter_dimension=1, tiled=True
    )
    return (activation, input_grad.astype(jnp.bfloat16), weight_grad)


def solution(mesh):
    on_ring = mesh.shape["dp"] == 2 * CHIPS and mesh.shape["bfly"] == 2
    return jax.shard_map(
        functools.partial(body, on_ring),
        mesh=mesh,
        in_specs=(P("dp", "bfly"), P(None, "dp", "bfly"), P(None, "bfly"), P("dp", "bfly")),
        out_specs=(P("dp", "bfly"), P("dp", "bfly"), P(None, "dp", "bfly")),
        check_vma=False,
    )
```
